256 devices in a mesh: dp: 16 (over y_lo, z), ctx: 16 (over y_hi, x, core).
Axes of the slice: x: 4, y: 4 (y_hi: 2, y_lo: 2; y = y_hi * 2 + y_lo), z: 8, core: 2. Of those that a mesh axis runs over, the one named last changes fastest.
Arguments:
- inputs: bfloat16 [16, 2048, 4096], P('dp', 'ctx'), may hold values from -6 to 6
- out_grads: bfloat16 [16, 2048, 1024], P('dp', 'ctx'), may hold values from -8 to 8
- basis_in: bfloat16 [4096, 4096], P(None, 'ctx'), may hold values from -0.09375 to 0.09375
- basis_out: bfloat16 [1024, 1024], replicated, may hold values from -0.1875 to 0.1875
Outputs:
- corrected: float32 [1024, 4096], P('dp', 'ctx')
The draws below stay inside these ranges and needn't reach their ends.
All inputs are finite; a program needn't handle non-finite values.
Results may differ from the reference program's by a relative error of at most 0.002.
Values may be sent and summed in bfloat16 or wider, within the bound.
A program may use at most 128 MiB of HBM per device.

```python
import jax
import jax.numpy as jnp
from jax import lax

D_IN = 4096
D_OUT = 1024
SEQ_LEN = 2048
SEQS = 16


def strengthened(drawn, own_key, source, target, parts, factor):
    owner, partner = [(jnp.arange(drawn.shape[position]) // (drawn.shape[position] // parts)).reshape([-1 if axis == position else 1 for axis in range(drawn.ndim)]) for position in (source, target)]
    chosen = jax.random.permutation(own_key, parts)[partner]
    strong = (owner == chosen) | (owner == (partner + parts // 2) % parts)
    return jnp.where(strong, factor * drawn, drawn)


def levels(key, shape, shards, low, top_value):
    factor_of = 1.0
    for dim, parts in shards:
        steps = jax.random.uniform(jax.random.fold_in(jax.random.fold_in(key, 6), dim), (parts,), jnp.float32, low / len(shards), top_value / len(shards))
        factor_of = factor_of * jnp.repeat(jnp.exp(steps), shape[dim] // parts).reshape((-1,) + (1,) * (len(shape) - 1 - dim))
    return factor_of


def normal_values(key, dims, scale, limit, split=(), dtype=jnp.bfloat16):
    result = jax.random.normal(key, dims, jnp.float32) * scale
    if len(split) > 0:
        result = levels(key, dims, split, -0.22, 0.18) * result
    return jnp.clip(result, min=-limit, max=limit).astype(dtype)


def gaussian_with(rng, extent, width, most, cuts, heavy, kind=jnp.bfloat16):
    values = width * jax.random.normal(rng, extent, jnp.float32)
    if cuts:
        values = values * levels(rng, extent, cuts, -0.22, 0.18)
    return jnp.clip(strengthened(values, jax.random.fold_in(rng, 3), *heavy), -most, most).astype(kind)


def setup_inputs(seed: int = 0) -> dict:
    key_list = jax.random.split(jax.random.key(seed), 5)
    return {
        "inputs": normal_values(key_list[0], (SEQS, SEQ_LEN, D_IN), 1.0, 6.0, ((0, 16), (1, 16))),
        "out_grads": gaussian_with(key_list[1], (SEQS, SEQ_LEN, D_OUT), 1.0, 8.0, ((0, 16), (1, 16)), (0, 2, 16, 2.0)),
        "basis_in": normal_values(key_list[2], (D_IN, D_IN), D_IN ** -0.5, 0.09375, ((1, 16),)),
        "basis_out": normal_values(key_list[3], (D_OUT, D_OUT), D_OUT ** -0.5, 0.1875),
    }


def reference(inputs, out_grads, basis_in, basis_out):
    def one_sequence(total, pair):
        acts, grads = pair
        rot_in = jnp.dot(acts, basis_in, preferred_element_type=jnp.float32).astype(jnp.bfloat16)
        rot_out = jnp.dot(grads, basis_out, preferred_element_type=jnp.float32).astype(jnp.bfloat16)
        tile = lax.dot_general(rot_out, rot_in, (((0,), (0,)), ((), ())), preferred_element_type=jnp.float32)
        return total + tile * tile, None

    start = jnp.zeros((out_grads.shape[2], inputs.shape[2]), jnp.float32)
    total, unused = lax.scan(one_sequence, start, (inputs, out_grads))
    return total / (SEQ_LEN * SEQS)
```

```python
import functools

import jax
import jax.numpy as jnp
from jax import lax
from jax.experimental import pallas as pl
from jax.experimental.pallas import tpu as pltpu
from jax.sharding import PartitionSpec as P

MESH = pl.DeviceIdType.MESH
BF16, F32 = jnp.bfloat16, jnp.float32
CHUNKS = ((0, 1), (1, 1), (2, 2), (4, 2), (6, 2))
GROUPS = ((0, 4), (4, 4))
N_SEND = 256
N_RECV = 256


class Sems:
    def __init__(self, send, recv):
        self.send, self.recv, self.n_send, self.slots = send, recv, 0, {}

    def out(self):
        self.n_send += 1
        return self.send.at[self.n_send - 1]

    def into(self, *name):
        return self.recv.at[self.slots.setdefault(name, len(self.slots))]


def kernel(
    scale, x_hbm, g_hbm, bi_hbm, bo_hbm, o_ref,
    xbuf, gbuf, bobuf, rbuf, rsend, psend, precv, pkeep, hz, hbuf, bbuf, acc, ssend, rr,
    send_sem, recv_sem, fin_sem,
):
    dp, ctx = lax.axis_index("dp"), lax.axis_index("ctx")
    yl, z = dp // 8, dp % 8
    a, b, c = ctx // 8, (ctx // 2) % 4, ctx % 2
    right, left = (b + 1) % 4, (b + 3) % 4
    sems = Sems(send_sem, recv_sem)
    pending = []

    def dev(a=a, yl=yl, z=z, b=b, c=c):
        return (yl * 8 + z, a * 8 + b * 2 + c)

    sibling = dev(c=1 - c)

    def send(src, dst, to, *name):
        copy = pltpu.make_async_remote_copy(
            src_ref=src, dst_ref=dst, send_sem=sems.out(), recv_sem=sems.into(*name),
            device_id=to, device_id_type=MESH,
        )
        copy.start()
        pending.append(copy)

    def wait(ref, *name):
        pltpu.make_async_copy(ref, ref, sems.into(*name)).wait()

    def local(src, dst, *name):
        copy = pltpu.make_async_copy(src, dst, sems.into(*name))
        copy.start()
        return copy

    def flush():
        while pending:
            pending.pop(0).wait_send()

    peers = [dev(b=(b + i) % 4, c=k) for i in (1, 3) for k in (0, 1)]
    peers += [dev(b=(b + 2) % 4), sibling]
    peers += [dev(z=(z + i) % 8) for i in range(1, 8)]
    peers += [
        dev(a=(a + i) % 2, yl=(yl + j) % 2, c=k)
        for i, j in ((0, 1), (1, 0), (1, 1))
        for k in (0, 1)
    ]
    barrier = pltpu.get_barrier_semaphore()
    for peer in peers:
        pl.semaphore_signal(barrier, inc=1, device_id=peer, device_id_type=MESH)
    own, partner = a * 2 + c, (1 - a) * 2 + c
    load_g = local(g_hbm.at[0], gbuf, "g")
    load_bo = local(bo_hbm, bobuf, "bo")
    features = pl.ds(pl.multiple_of(b * 1024, 1024), 1024)
    load_x = local(x_hbm.at[0, :, features], xbuf.at[c, b], "x")
    load_bi = local(bi_hbm, bbuf.at[own], "bi")
    pl.semaphore_wait(barrier, len(peers))

    def x_send(j):
        lo, n = CHUNKS[j]
        for i in (1, 3, 2):
            to = (b + i) % 4
            src = pl.ds(pl.multiple_of(to * 1024 + lo * 128, 128), n * 128)
            send(
                x_hbm.at[0, :, src], xbuf.at[c, b, :, pl.ds(lo * 128, n * 128)],
                dev(b=to), "X", j, i,
            )

    def b_send(g):
        lo, n = GROUPS[g]
        at = (pl.ds(2 * (1 - yl), 2), pl.ds(lo * 128, n * 128))
        send(bi_hbm.at[at], bbuf.at[(own, *at)], dev(a=1 - a, yl=1 - yl), "B1", g)

    def b_forward(g):
        lo, n = GROUPS[g]
        at = (partner, pl.ds(2 * yl, 2), pl.ds(lo * 128, n * 128))
        wait(bbuf.at[at], "B1", g)
        send(bbuf.at[at], bbuf.at[at], dev(yl=1 - yl), "B2", g)

    def b_share(g):
        lo, n = GROUPS[g]
        at = (partner, pl.ds(2 * (1 - yl), 2), pl.ds(lo * 128, n * 128))
        wait(bbuf.at[at], "B2", g)
        at = (partner, slice(None), pl.ds(lo * 128, n * 128))
        send(bbuf.at[at], bbuf.at[at], sibling, "B3", g)

    def b_done(g):
        lo, n = GROUPS[g]
        wait(bbuf.at[(3 - own) % 4, :, pl.ds(lo * 128, n * 128)], "B3", g)

    x_send(0)
    b_send(0)

    load_g.wait()
    load_bo.wait()
    for k in range(2):
        rot = jnp.dot(gbuf[...], bobuf[:, 512 * k : 512 * k + 512], preferred_element_type=F32)
        turned = rot.T.astype(BF16).reshape(8, 2, 32, 128)
        for h in range(2):
            rsend[k, h] = turned[:, h].reshape(256, 128)
    slot = c * 4 + b
    for i in (1, 3):
        to = (b + i) % 4
        send(rsend.at[c], rbuf.at[slot], dev(b=to), "R", i, 0)
        send(rsend.at[1 - c], rbuf.at[slot], dev(b=to, c=1 - c), "R", i, 1)
    send(rsend.at[1 - c], rbuf.at[slot], sibling, "R", 0, 1)
    rbuf[slot] = rsend[c]
    send(bi_hbm, bbuf.at[own], sibling, "B0")
    x_send(1)

    def r_forward(i, origin, to):
        same, other = c * 4 + origin, (1 - c) * 4 + origin
        wait(rbuf.at[same], "R", i, 0)
        wait(rbuf.at[other], "R", i, 1)
        first = 0 if i == 1 else 4
        send(rbuf.at[first + origin], rbuf.at[first + origin], dev(b=to), "R", 2, i)

    r_forward(1, left, right)
    r_forward(3, right, left)
    x_send(2)
    b_forward(0)
    x_send(3)
    x_send(4)
    far = (b + 2) % 4
    wait(rbuf.at[far], "R", 2, 1)
    wait(rbuf.at[4 + far], "R", 2, 3)
    wait(rbuf.at[(1 - c) * 4 + b], "R", 0, 1)
    load_x.wait()

    def A(j):
        lo, n = CHUNKS[j]
        columns = pl.ds(lo * 128, n * 128)
        for i in (1, 3, 2):
            wait(xbuf.at[c, (b + 4 - i) % 4, :, columns], "X", j, i)
        at = (c, slice(None), slice(None), columns)
        send(xbuf.at[at], xbuf.at[at], sibling, "XF", j)

    def B(j):
        lo, n = CHUNKS[j]
        columns = pl.ds(lo * 128, n * 128)
        wait(xbuf.at[1 - c, :, :, columns], "XF", j)

        def product(half):
            lhs = jnp.concatenate([rbuf[s, half] for s in range(8)], axis=1)
            rhs = xbuf[:, :, :, lo * 128 : (lo + n) * 128].reshape(1024, n * 128)
            return jnp.dot(lhs, rhs, preferred_element_type=F32)

        theirs = product(1 - a).astype(BF16)
        for i in range(n):
            psend[lo + i] = theirs[:, i * 128 : (i + 1) * 128]
        at = pl.ds(lo, n)
        send(psend.at[at], precv.at[at], dev(a=1 - a), "P", j)
        mine = product(a)
        for i in range(n):
            pkeep[lo + i] = mine[:, i * 128 : (i + 1) * 128]

    def C(j):
        lo, n = CHUNKS[j]
        at = pl.ds(lo, n)
        wait(precv.at[at], "P", j)
        hz[lo : lo + n] = (pkeep[lo : lo + n] + precv[lo : lo + n].astype(F32)).astype(BF16)
        rows = pl.ds(pl.multiple_of(z * 32, 32), 32)
        for i in (4, 3, 5, 2, 6, 1, 7):
            to = (z + i) % 8
            theirs = pl.ds(pl.multiple_of(to * 32, 32), 32)
            send(hz.at[at, theirs], hbuf.at[b, at, rows], dev(z=to), "Z", j, i)
        for i in range(n):
            hbuf[b, lo + i, rows] = hz[lo + i, rows]

    def D(j):
        lo, n = CHUNKS[j]
        at = pl.ds(lo, n)
        for i in range(1, 8):
            rows = pl.ds(pl.multiple_of((z + 8 - i) % 8 * 32, 32), 32)
            wait(hbuf.at[b, at, rows], "Z", j, i)
        send(hbuf.at[b, at], hbuf.at[b, at], dev(b=right), "H", j, 1)
        send(hbuf.at[b, at], hbuf.at[b, at], dev(b=left), "H", j, 3)

    def E(j):
        lo, n = CHUNKS[j]
        at = pl.ds(lo, n)
        wait(hbuf.at[left, at], "H", j, 1)
        half = hbuf.at[left, at, pl.ds(0, 128)]
        send(half, half, dev(b=right), "HF", j, 1)
        wait(hbuf.at[right, at], "H", j, 3)
        half = hbuf.at[right, at, pl.ds(128, 128)]
        send(half, half, dev(b=left), "HF", j, 3)

    def F(j):
        lo, n = CHUNKS[j]
        at = pl.ds(lo, n)
        wait(hbuf.at[far, at, pl.ds(0, 128)], "HF", j, 1)
        wait(hbuf.at[far, at, pl.ds(128, 128)], "HF", j, 3)
        lhs = jnp.concatenate(
            [hbuf[x, lo + i] for x in range(4) for i in range(n)], axis=1
        )
        for k in range(4):
            rhs = bbuf[k, :, lo * 128 : (lo + n) * 128].reshape(n * 512, 256)
            term = jnp.dot(lhs, rhs, preferred_element_type=F32)
            acc[k] = term if j == 0 else acc[k] + term

    A(0)
    B(0)
    A(1)
    B(1)
    C(0)
    A(2)
    B(2)
    C(1)
    D(0)
    A(3)
    B(3)
    C(2)
    D(1)
    A(4)
    B(4)
    b_send(1)
    b_share(0)
    E(0)
    C(3)
    D(2)
    E(1)
    C(4)
    load_bi.wait()
    wait(bbuf.at[a * 2 + 1 - c], "B0")
    b_done(0)
    F(0)
    D(3)
    F(1)
    E(2)
    b_forward(1)
    D(4)
    b_share(1)
    F(2)
    E(3)
    b_done(1)
    F(3)
    E(4)
    flush()
    F(4)

    for k in range(4):
        tile = acc[k]
        ssend[k] = (tile * tile).reshape(8, 32, 256).sum(axis=0) * scale
    for i in range(2):
        for k in range(2):
            mine = (a == i) & (c == k) & (yl == c)
            copy = pltpu.make_async_remote_copy(
                src_ref=ssend.at[2 * i + k], dst_ref=rr.at[2 * a + yl],
                send_sem=sems.out(), recv_sem=fin_sem.at[2 * a + yl],
                device_id=dev(a=i, yl=c, c=k), device_id_type=MESH,
            )

            @pl.when(mine)
            def _():
                rr[2 * i + k] = ssend[2 * i + k]

            @pl.when(jnp.logical_not(mine))
            def _(copy=copy):
                copy.start()

            pending.append((mine, copy))
    for i in range(2):
        for k in range(2):
            mine = (a == i) & (c == yl) & (yl == k)

            @pl.when(jnp.logical_not(mine))
            def _():
                at = rr.at[2 * i + k]
                pltpu.make_async_copy(at, at, fin_sem.at[2 * i + k]).wait()

        o_ref[32 * i : 32 * i + 32] = rr[2 * i] + rr[2 * i + 1]
    for mine, copy in pending:

        @pl.when(jnp.logical_not(mine))
        def _(copy=copy):
            copy.wait_send()


def local(inputs, out_grads, basis_in, basis_out):
    scale = 1.0 / (inputs.shape[1] * lax.axis_size("ctx") * inputs.shape[0] * lax.axis_size("dp"))
    anywhere = pl.BlockSpec(memory_space=pl.ANY)
    return pl.pallas_call(
        functools.partial(kernel, scale),
        out_shape=jax.ShapeDtypeStruct((64, 256), F32),
        in_specs=[anywhere] * 4,
        out_specs=pl.BlockSpec(memory_space=pltpu.VMEM),
        scratch_shapes=[
            pltpu.VMEM((2, 4, 128, 1024), BF16),
            pltpu.VMEM((128, 1024), BF16),
            pltpu.VMEM((1024, 1024), BF16),
            pltpu.VMEM((8, 2, 256, 128), BF16),
            pltpu.VMEM((2, 2, 256, 128), BF16),
            pltpu.VMEM((8, 256, 128), BF16),
            pltpu.VMEM((8, 256, 128), BF16),
            pltpu.VMEM((8, 256, 128), F32),
            pltpu.VMEM((8, 256, 128), BF16),
            pltpu.VMEM((4, 8, 256, 128), BF16),
            pltpu.VMEM((4, 4, 1024, 256), BF16),
            pltpu.VMEM((4, 256, 256), F32),
            pltpu.VMEM((4, 32, 256), F32),
            pltpu.VMEM((4, 32, 256), F32),
            pltpu.SemaphoreType.DMA((N_SEND,)),
            pltpu.SemaphoreType.DMA((N_RECV,)),
            pltpu.SemaphoreType.DMA((4,)),
        ],
        compiler_params=pltpu.CompilerParams(
            collective_id=0, has_side_effects=True, vmem_limit_bytes=48 << 20
        ),
    )(inputs, out_grads, basis_in.reshape(4, 1024, 256), basis_out)


def solution(mesh):
    return jax.shard_map(
        local,
        mesh=mesh,
        in_specs=(P("dp", "ctx", None), P("dp", "ctx", None), P(None, "ctx"), P()),
        out_specs=P("dp", "ctx"),
        check_vma=False,
    )
```

```python
import functools
import math

import jax
import jax.numpy as jnp
from jax import lax
from jax.experimental import pallas as pl
from jax.experimental.pallas import tpu as pltpu
from jax.sharding import PartitionSpec as P

MESH = pl.DeviceIdType.MESH
BF16, F32 = jnp.bfloat16, jnp.float32
BLOCKS = 8
PIECES = 8
EARLY = 6
DIRECT = (6, 7)
N_SEND = 12
N_RECV = 80
VMEM = 63 << 20


def size(ref):
    return math.prod(ref.shape) * ref.dtype.itemsize


def kernel(
    scale, x_hbm, g_hbm, bi_hbm, bo_hbm, o_ref,
    xbuf, gbuf, bobuf, rbuf, rsend, psend, precv, pkeep, hz, hbuf, bbuf, acc, ssend, rr,
    send_sem, recv_sem, fin_sem,
):
    dp, ctx = lax.axis_index("dp"), lax.axis_index("ctx")
    yl, z = dp // 8, dp % 8
    a, b, c = ctx // 8, (ctx // 2) % 4, ctx % 2
    right, left, far = (b + 1) % 4, (b + 3) % 4, (b + 2) % 4
    own, partner = a * 2 + c, (1 - a) * 2 + c
    senders, receivers, sent, due = {}, {}, {}, {}

    def dev(a=a, yl=yl, z=z, b=b, c=c):
        return (yl * 8 + z, a * 8 + b * 2 + c)

    sibling = dev(c=1 - c)

    def out(kind):
        return send_sem.at[senders.setdefault(kind, len(senders))]

    def into(name):
        return recv_sem.at[receivers.setdefault(name, len(receivers))]

    def send(src, dst, to, *name):
        pltpu.make_async_remote_copy(
            src_ref=src, dst_ref=dst, send_sem=out(name[0]), recv_sem=into(name),
            device_id=to, device_id_type=MESH,
        ).start()
        sent[name[0]] = sent.get(name[0], 0) + size(src)
        due.setdefault(name, []).append(dst)

    def wait(ref, *name):
        assert size(ref) == sum(map(size, due.pop(name))), name
        pltpu.make_async_copy(ref, ref, into(name)).wait()

    def wait_sent(ref, kind):
        assert size(ref) == sent.pop(kind), kind
        pltpu.make_async_remote_copy(
            src_ref=ref, dst_ref=ref, send_sem=out(kind), recv_sem=recv_sem.at[0],
            device_id=sibling, device_id_type=MESH,
        ).wait_send()

    def local(src, dst, name):
        copy = pltpu.make_async_copy(src, dst, into(name))
        copy.start()
        return copy

    peers = [dev(b=(b + i) % 4, c=k) for i in (1, 3) for k in (0, 1)]
    peers += [dev(b=far), sibling]
    peers += [dev(z=(z + i) % 8) for i in range(1, 8)]
    peers += [
        dev(a=(a + i) % 2, yl=(yl + j) % 2, c=k)
        for i, j in ((0, 1), (1, 0), (1, 1))
        for k in (0, 1)
    ]
    barrier = pltpu.get_barrier_semaphore()
    for peer in peers:
        pl.semaphore_signal(barrier, inc=1, device_id=peer, device_id_type=MESH)
    features = pl.ds(pl.multiple_of(b * 1024, 1024), 1024)
    load_g = local(g_hbm.at[0], gbuf, "g")
    load_bo = local(bo_hbm, bobuf, "bo")
    load_x = local(x_hbm.at[0, :, features], xbuf.at[c, b], "x")
    load_bi = local(bi_hbm, bbuf.at[own], "bi")
    pl.semaphore_wait(barrier, len(peers))

    def at_lanes(j):
        return pl.ds(j * 128, 128)

    def at_rows(k):
        return pl.ds(pl.multiple_of(k * 32, 32), 32)

    def x_send(j):
        for to in (right, left, far):
            src = pl.ds(pl.multiple_of(to * 1024 + j * 128, 128), 128)
            send(x_hbm.at[0, :, src], xbuf.at[c, b, :, at_lanes(j)], dev(b=to), "X", j)

    def x_share(j):
        wait(xbuf.at[0, pl.ds(0, 3), :, at_lanes(j)], "X", j)
        at = (c, slice(None), slice(None), at_lanes(j))
        send(xbuf.at[at], xbuf.at[at], sibling, "XF", j)

    def b_at(k, g):
        rows = 1024 // PIECES
        return (2 * (z % 2) + k, pl.ds(g * rows, rows))

    def b_send(g):
        at = b_at(1 - yl, g)
        send(bi_hbm.at[at], bbuf.at[(own, *at)], dev(a=1 - a, yl=1 - yl), "B1", g)

    def b_forward(g):
        ref = bbuf.at[(partner, *b_at(yl, g))]
        wait(ref, "B1", g)
        send(ref, ref, dev(yl=1 - yl), "B2", g)
        send(ref, ref, dev(z=(z + 9 - 2 * yl) % 8), "BZ", int(g >= EARLY))

    def b_relay(g):
        ref = bbuf.at[(partner, *b_at(1 - yl, g))]
        wait(ref, "B2", g)
        send(ref, ref, dev(z=(z + 7 + 2 * yl) % 8), "BZ", int(g >= EARLY))

    def b_rows(h):
        rows = 1024 // PIECES
        return pl.ds(EARLY * rows, 1024 - EARLY * rows) if h else pl.ds(0, EARLY * rows)

    def b_share(h):
        wait(bbuf.at[partner, pl.ds(0, 2), b_rows(h)], "BZ", h)
        ref = bbuf.at[partner, :, b_rows(h)]
        send(ref, ref, sibling, "B3", h)

    def b_done(h):
        wait(bbuf.at[3 - own, :, b_rows(h)], "B3", h)

    def b_own_done():
        load_bi.wait()
        wait(bbuf.at[a * 2 + 1 - c], "B0")

    def b_own():
        send(bi_hbm, bbuf.at[own], sibling, "B0")

    slot = c * 4 + b

    def r_compute():
        load_g.wait()
        load_bo.wait()
        for k in range(2):
            rot = jnp.dot(
                gbuf[...], bobuf[:, 512 * k : 512 * k + 512], preferred_element_type=F32
            )
            turned = rot.T.astype(BF16).reshape(8, 2, 32, 128)
            for h in range(2):
                rsend[k, h] = turned[:, h].reshape(256, 128)

    def half(p):
        return a if p else 1 - a

    def r_send(p):
        h = half(p)
        for i, to in ((1, right), (3, left)):
            send(rsend.at[c, h], rbuf.at[slot, h], dev(b=to), "R", p, i)
            send(rsend.at[1 - c, h], rbuf.at[slot, h], dev(b=to, c=1 - c), "R", p, i)
        send(rsend.at[1 - c, h], rbuf.at[slot, h], sibling, "R", p, 2)
        rbuf[slot, h] = rsend[c, h]

    def r_forward(p):
        h = half(p)
        for i, origin, to, first in ((1, left, right, 0), (3, right, left, 4)):
            wait(rbuf.at[pl.ds(0, 2), 0], "R", p, i)
            block = rbuf.at[first + origin, h]
            send(block, block, dev(b=to), "R", p, 2)

    def r_done(p):
        wait(rbuf.at[pl.ds(0, 3), 0], "R", p, 2)

    def product(j, h):
        lhs = jnp.concatenate([rbuf[s, h] for s in range(8)], axis=1)
        rhs = xbuf[:, :, :, j * 128 : j * 128 + 128].reshape(1024, 128)
        return jnp.dot(lhs, rhs, preferred_element_type=F32)

    def theirs(j):
        wait(xbuf.at[1 - c, :, :, at_lanes(j)], "XF", j)
        psend[j] = product(j, 1 - a).astype(BF16)
        send(psend.at[j], precv.at[j], dev(a=1 - a), "P", j)

    def mine(j):
        pkeep[j] = product(j, a)

    def z_send(j):
        wait(precv.at[j], "P", j)
        hz[j] = (pkeep[j] + precv[j].astype(F32)).astype(BF16)
        for i in (4, 3, 5, 2, 6, 1, 7):
            to = (z + i) % 8
            send(hz.at[j, at_rows(to)], hbuf.at[b, j, at_rows(z)], dev(z=to), "Z", j)
        hbuf[b, j, at_rows(z)] = hz[j, at_rows(z)]

    def h_send(j):
        wait(hbuf.at[b, j, pl.ds(0, 224)], "Z", j)
        ref = hbuf.at[b, j]
        if j in DIRECT:
            send(ref, ref, dev(b=far), "HF", j)
        for to in (right, left):
            send(ref, ref, dev(b=to), "H", j)

    def h_wait(j):
        wait(hbuf.at[pl.ds(0, 2), j], "H", j)

    def h_forward(j):
        h_wait(j)
        for origin, to, first in ((left, right, 0), (right, left, 128)):
            part = hbuf.at[origin, j, pl.ds(first, 128)]
            send(part, part, dev(b=to), "HF", j)

    def tile_begin(j):
        if j in DIRECT:
            h_wait(j)
        wait(hbuf.at[far, j], "HF", j)
        return jnp.concatenate([hbuf[x, j] for x in range(4)], axis=1)

    def tile_term(j, k, lhs):
        rhs = bbuf[k, :, j * 128 : j * 128 + 128].reshape(512, 256)
        return jnp.dot(lhs, rhs, preferred_element_type=F32)

    def tile(j):
        lhs = tile_begin(j)
        for k in range(4):
            term = tile_term(j, k, lhs)
            acc[k] = term if j == 0 else acc[k] + term

    def wait_all_sent():
        wait_sent(xbuf.at[0, pl.ds(0, 3)], "X")
        wait_sent(xbuf.at[0], "XF")
        wait_sent(rbuf.at[pl.ds(0, 7)], "R")
        wait_sent(psend, "P")
        wait_sent(hz.at[pl.ds(0, 7)], "Z")
        wait_sent(hbuf.at[pl.ds(0, 2)], "H")
        wait_sent(hbuf.at[0], "HF")
        wait_sent(bbuf.at[0], "B0")
        wait_sent(bbuf.at[0, 0], "B1")
        wait_sent(bbuf.at[0, 0], "B2")
        wait_sent(bbuf.at[0, pl.ds(0, 2)], "BZ")
        wait_sent(bbuf.at[0], "B3")

    x_send(0)
    b_send(0)
    b_send(1)
    b_send(2)
    b_send(3)
    b_send(4)
    b_send(5)
    r_compute()
    r_send(0)
    r_send(1)
    b_own()
    load_x.wait()
    x_share(0)
    b_forward(0)
    r_forward(0)
    x_send(1)
    x_send(2)
    b_forward(1)
    b_forward(2)
    b_forward(3)
    b_relay(0)
    r_forward(1)
    x_send(3)
    x_send(4)
    x_send(5)
    x_send(6)
    x_send(7)
    b_forward(4)
    b_relay(1)
    r_done(0)
    theirs(0)
    b_forward(5)
    b_relay(2)
    x_share(1)
    theirs(1)
    b_relay(3)
    x_share(2)
    theirs(2)
    b_relay(4)
    r_done(1)
    mine(0)
    mine(1)
    b_relay(5)
    z_send(0)
    x_share(3)
    theirs(3)
    mine(2)
    z_send(1)
    x_share(4)
    theirs(4)
    mine(3)
    x_share(5)
    z_send(2)
    theirs(5)
    mine(4)
    h_send(0)
    x_share(6)
    h_send(1)
    theirs(6)
    mine(5)
    x_share(7)
    z_send(3)
    theirs(7)
    b_send(6)
    b_send(7)
    z_send(4)
    mine(6)
    h_send(2)
    mine(7)
    z_send(5)
    b_share(0)
    h_forward(0)
    z_send(6)
    h_send(3)
    h_forward(1)
    b_forward(6)
    z_send(7)
    h_send(4)
    b_forward(7)
    h_forward(2)
    b_own_done()
    b_done(0)
    tile(0)
    h_send(5)
    h_send(6)
    h_forward(3)
    b_relay(6)
    tile(1)
    h_send(7)
    b_relay(7)
    h_forward(4)
    tile(2)
    h_forward(5)
    b_share(1)
    tile(3)
    tile(4)
    tile(5)
    b_done(1)
    wait_all_sent()
    tile(6)

    copies = []
    last = tile_begin(BLOCKS - 1)
    for i in range(2):
        for k in range(2):
            part = acc[2 * i + k] + tile_term(BLOCKS - 1, 2 * i + k, last)
            ssend[2 * i + k] = (part * part).reshape(8, 32, 256).sum(axis=0) * scale
            stays = (a == i) & (c == k) & (yl == c)
            copy = pltpu.make_async_remote_copy(
                src_ref=ssend.at[2 * i + k], dst_ref=rr.at[2 * a + yl],
                send_sem=fin_sem.at[4 + 2 * i + k], recv_sem=fin_sem.at[2 * a + yl],
                device_id=dev(a=i, yl=c, c=k), device_id_type=MESH,
            )
            copies.append((stays, copy))

            @pl.when(stays)
            def _():
                rr[2 * i + k] = ssend[2 * i + k]

            @pl.when(jnp.logical_not(stays))
            def _():
                copy.start()

    for i in range(2):
        for k in range(2):

            @pl.when(jnp.logical_not((a == i) & (c == yl) & (yl == k)))
            def _():
                at = rr.at[2 * i + k]
                pltpu.make_async_copy(at, at, fin_sem.at[2 * i + k]).wait()

        o_ref[32 * i : 32 * i + 32] = rr[2 * i] + rr[2 * i + 1]
    for stays, copy in copies:

        @pl.when(jnp.logical_not(stays))
        def _():
            copy.wait_send()


def local(inputs, out_grads, basis_in, basis_out):
    scale = 1.0 / (inputs.shape[1] * lax.axis_size("ctx") * inputs.shape[0] * lax.axis_size("dp"))
    anywhere = pl.BlockSpec(memory_space=pl.ANY)
    return pl.pallas_call(
        functools.partial(kernel, scale),
        out_shape=jax.ShapeDtypeStruct((64, 256), F32),
        in_specs=[anywhere] * 4,
        out_specs=pl.BlockSpec(memory_space=pltpu.VMEM),
        scratch_shapes=[
            pltpu.VMEM((2, 4, 128, 1024), BF16),
            pltpu.VMEM((128, 1024), BF16),
            pltpu.VMEM((1024, 1024), BF16),
            pltpu.VMEM((8, 2, 256, 128), BF16),
            pltpu.VMEM((2, 2, 256, 128), BF16),
            pltpu.VMEM((8, 256, 128), BF16),
            pltpu.VMEM((8, 256, 128), BF16),
            pltpu.VMEM((8, 256, 128), F32),
            pltpu.VMEM((8, 256, 128), BF16),
            pltpu.VMEM((4, 8, 256, 128), BF16),
            pltpu.VMEM((4, 4, 1024, 256), BF16),
            pltpu.VMEM((4, 256, 256), F32),
            pltpu.VMEM((4, 32, 256), F32),
            pltpu.VMEM((4, 32, 256), F32),
            pltpu.SemaphoreType.DMA((N_SEND,)),
            pltpu.SemaphoreType.DMA((N_RECV,)),
            pltpu.SemaphoreType.DMA((8,)),
        ],
        compiler_params=pltpu.CompilerParams(
            collective_id=0, has_side_effects=True, vmem_limit_bytes=VMEM
        ),
    )(inputs, out_grads, basis_in.reshape(4, 1024, 256), basis_out)


def solution(mesh):
    return jax.shard_map(
        local,
        mesh=mesh,
        in_specs=(P("dp", "ctx", None), P("dp", "ctx", None), P(None, "ctx"), P()),
        out_specs=P("dp", "ctx"),
        check_vma=False,
    )
```

```python
import functools
import math

import jax
import jax.numpy as jnp
from jax import lax
from jax.experimental import pallas as pl
from jax.experimental.pallas import tpu as pltpu
from jax.sharding import PartitionSpec as P

MESH = pl.DeviceIdType.MESH
BF16, F32 = jnp.bfloat16, jnp.float32
BLOCKS = 8
PIECES = 8
EARLY = 6
DIRECT = (7,)
N_SEND = 12
N_RECV = 80
VMEM = 54976 << 10


def size(ref):
    return math.prod(ref.shape) * ref.dtype.itemsize


def kernel(
    scale, x_hbm, g_hbm, bi_hbm, bo_hbm, o_ref,
    xbuf, gbuf, bobuf, rbuf, rsend, psend, precv, pkeep, hz, hbuf, bbuf, acc, ssend, rr,
    send_sem, recv_sem, fin_sem,
):
    dp, ctx = lax.axis_index("dp"), lax.axis_index("ctx")
    yl, z = dp // 8, dp % 8
    a, b, c = ctx // 8, (ctx // 2) % 4, ctx % 2
    right, left, far = (b + 1) % 4, (b + 3) % 4, (b + 2) % 4
    own, partner = a * 2 + c, (1 - a) * 2 + c
    senders, receivers, sent, due = {}, {}, {}, {}

    def dev(a=a, yl=yl, z=z, b=b, c=c):
        return (yl * 8 + z, a * 8 + b * 2 + c)

    sibling = dev(c=1 - c)

    def out(kind):
        return send_sem.at[senders.setdefault(kind, len(senders))]

    def into(name):
        return recv_sem.at[receivers.setdefault(name, len(receivers))]

    def send(src, dst, to, *name):
        pltpu.make_async_remote_copy(
            src_ref=src, dst_ref=dst, send_sem=out(name[0]), recv_sem=into(name),
            device_id=to, device_id_type=MESH,
        ).start()
        sent[name[0]] = sent.get(name[0], 0) + size(src)
        due.setdefault(name, []).append(dst)

    def wait(ref, *name):
        assert size(ref) == sum(map(size, due.pop(name))), name
        pltpu.make_async_copy(ref, ref, into(name)).wait()

    def wait_sent(ref, kind):
        assert size(ref) == sent.pop(kind), kind
        pltpu.make_async_remote_copy(
            src_ref=ref, dst_ref=ref, send_sem=out(kind), recv_sem=recv_sem.at[0],
            device_id=sibling, device_id_type=MESH,
        ).wait_send()

    def local(src, dst, name):
        copy = pltpu.make_async_copy(src, dst, into(name))
        copy.start()
        return copy

    peers = [dev(b=(b + i) % 4, c=k) for i in (1, 3) for k in (0, 1)]
    peers += [dev(b=far), sibling]
    peers += [dev(z=(z + i) % 8) for i in range(1, 8)]
    peers += [
        dev(a=(a + i) % 2, yl=(yl + j) % 2, c=k)
        for i, j in ((0, 1), (1, 0), (1, 1))
        for k in (0, 1)
    ]
    barrier = pltpu.get_barrier_semaphore()
    for peer in peers:
        pl.semaphore_signal(barrier, inc=1, device_id=peer, device_id_type=MESH)
    features = pl.ds(pl.multiple_of(b * 1024, 1024), 1024)
    load_g = local(g_hbm.at[0], gbuf, "g")
    load_bo = local(bo_hbm, bobuf, "bo")
    load_x = local(x_hbm.at[0, :, features], xbuf.at[c, b], "x")
    load_bi = local(bi_hbm, bbuf.at[own], "bi")
    pl.semaphore_wait(barrier, len(peers))

    def at_lanes(j):
        return pl.ds(j * 128, 128)

    def at_rows(k):
        return pl.ds(pl.multiple_of(k * 32, 32), 32)

    def x_send(j):
        for to in (right, left, far):
            src = pl.ds(pl.multiple_of(to * 1024 + j * 128, 128), 128)
            send(x_hbm.at[0, :, src], xbuf.at[c, b, :, at_lanes(j)], dev(b=to), "X", j)

    def x_share(j):
        wait(xbuf.at[0, pl.ds(0, 3), :, at_lanes(j)], "X", j)
        at = (c, slice(None), slice(None), at_lanes(j))
        send(xbuf.at[at], xbuf.at[at], sibling, "XF", j)

    def b_at(k, g):
        rows = 1024 // PIECES
        return (2 * (z % 2) + k, pl.ds(g * rows, rows))

    def b_send(g):
        at = b_at(1 - yl, g)
        send(bi_hbm.at[at], bbuf.at[(own, *at)], dev(a=1 - a, yl=1 - yl), "B1", g)

    def b_forward(g):
        ref = bbuf.at[(partner, *b_at(yl, g))]
        wait(ref, "B1", g)
        send(ref, ref, dev(yl=1 - yl), "B2", g)
        send(ref, ref, dev(z=(z + 9 - 2 * yl) % 8), "BZ", int(g >= EARLY))

    def b_relay(g):
        ref = bbuf.at[(partner, *b_at(1 - yl, g))]
        wait(ref, "B2", g)
        send(ref, ref, dev(z=(z + 7 + 2 * yl) % 8), "BZ", int(g >= EARLY))

    def b_rows(h):
        rows = 1024 // PIECES
        return pl.ds(EARLY * rows, 1024 - EARLY * rows) if h else pl.ds(0, EARLY * rows)

    def b_share(h):
        wait(bbuf.at[partner, pl.ds(0, 2), b_rows(h)], "BZ", h)
        ref = bbuf.at[partner, :, b_rows(h)]
        send(ref, ref, sibling, "B3", h)

    def b_done(h):
        wait(bbuf.at[3 - own, :, b_rows(h)], "B3", h)

    def b_own_done():
        load_bi.wait()
        wait(bbuf.at[a * 2 + 1 - c], "B0")

    def b_own():
        send(bi_hbm, bbuf.at[own], sibling, "B0")

    slot = c * 4 + b

    def r_compute():
        load_g.wait()
        load_bo.wait()
        for k in range(2):
            rot = jnp.dot(
                gbuf[...], bobuf[:, 512 * k : 512 * k + 512], preferred_element_type=F32
            )
            turned = rot.T.astype(BF16).reshape(8, 2, 32, 128)
            for h in range(2):
                rsend[k, h] = turned[:, h].reshape(256, 128)

    def half(p):
        return a if p else 1 - a

    def r_send(p):
        h = half(p)
        for i, to in ((1, right), (3, left)):
            send(rsend.at[c, h], rbuf.at[slot, h], dev(b=to), "R", p, i)
            send(rsend.at[1 - c, h], rbuf.at[slot, h], dev(b=to, c=1 - c), "R", p, i)
        send(rsend.at[1 - c, h], rbuf.at[slot, h], sibling, "R", p, 2)
        rbuf[slot, h] = rsend[c, h]

    def r_forward(p):
        h = half(p)
        for i, origin, to, first in ((1, left, right, 0), (3, right, left, 4)):
            wait(rbuf.at[pl.ds(0, 2), 0], "R", p, i)
            block = rbuf.at[first + origin, h]
            send(block, block, dev(b=to), "R", p, 2)

    def r_done(p):
        wait(rbuf.at[pl.ds(0, 3), 0], "R", p, 2)

    def product(j, h):
        lhs = jnp.concatenate([rbuf[s, h] for s in range(8)], axis=1)
        rhs = xbuf[:, :, :, j * 128 : j * 128 + 128].reshape(1024, 128)
        return jnp.dot(lhs, rhs, preferred_element_type=F32)

    def theirs(j):
        wait(xbuf.at[1 - c, :, :, at_lanes(j)], "XF", j)
        psend[j] = product(j, 1 - a).astype(BF16)
        send(psend.at[j], precv.at[j], dev(a=1 - a), "P", j)

    def mine(j):
        pkeep[j] = product(j, a)

    def z_send(j):
        wait(precv.at[j], "P", j)
        hz[j] = (pkeep[j] + precv[j].astype(F32)).astype(BF16)
        for i in (4, 3, 5, 2, 6, 1, 7):
            to = (z + i) % 8
            send(hz.at[j, at_rows(to)], hbuf.at[b, j, at_rows(z)], dev(z=to), "Z", j)
        hbuf[b, j, at_rows(z)] = hz[j, at_rows(z)]

    def h_send(j):
        wait(hbuf.at[b, j, pl.ds(0, 224)], "Z", j)
        ref = hbuf.at[b, j]
        if j in DIRECT:
            send(ref, ref, dev(b=far), "HF", j)
        for to in (right, left):
            send(ref, ref, dev(b=to), "H", j)

    def h_wait(j):
        wait(hbuf.at[pl.ds(0, 2), j], "H", j)

    def h_forward(j):
        h_wait(j)
        for origin, to, first in ((left, right, 0), (right, left, 128)):
            part = hbuf.at[origin, j, pl.ds(first, 128)]
            send(part, part, dev(b=to), "HF", j)

    def tile_begin(j):
        if j in DIRECT:
            h_wait(j)
        wait(hbuf.at[far, j], "HF", j)
        return jnp.concatenate([hbuf[x, j] for x in range(4)], axis=1)

    def tile_term(j, k, lhs):
        rhs = bbuf[k, :, j * 128 : j * 128 + 128].reshape(512, 256)
        return jnp.dot(lhs, rhs, preferred_element_type=F32)

    def tile(j):
        lhs = tile_begin(j)
        for k in range(4):
            term = tile_term(j, k, lhs)
            acc[k] = term if j == 0 else acc[k] + term

    def wait_all_sent():
        wait_sent(xbuf.at[0, pl.ds(0, 3)], "X")
        wait_sent(xbuf.at[0], "XF")
        wait_sent(rbuf.at[pl.ds(0, 7)], "R")
        wait_sent(psend, "P")
        wait_sent(hz.at[pl.ds(0, 7)], "Z")
        wait_sent(hbuf.at[pl.ds(0, 2)], "H")
        wait_sent(hbuf.at[0], "HF")
        wait_sent(bbuf.at[0], "B0")
        wait_sent(bbuf.at[0, 0], "B1")
        wait_sent(bbuf.at[0, 0], "B2")
        wait_sent(bbuf.at[0, pl.ds(0, 2)], "BZ")
        wait_sent(bbuf.at[0], "B3")

    x_send(0)
    b_send(0)
    b_send(1)
    b_send(2)
    b_send(3)
    b_send(4)
    b_send(5)
    r_compute()
    r_send(0)
    r_send(1)
    b_own()
    load_x.wait()
    x_share(0)
    b_forward(0)
    r_forward(0)
    x_send(1)
    x_send(2)
    b_forward(1)
    b_forward(2)
    b_forward(3)
    b_relay(0)
    r_forward(1)
    x_send(3)
    x_send(4)
    x_send(5)
    x_send(6)
    x_send(7)
    b_forward(4)
    b_relay(1)
    r_done(0)
    theirs(0)
    b_forward(5)
    b_relay(2)
    x_share(1)
    theirs(1)
    b_relay(3)
    x_share(2)
    theirs(2)
    b_relay(4)
    r_done(1)
    mine(0)
    mine(1)
    b_relay(5)
    z_send(0)
    x_share(3)
    theirs(3)
    mine(2)
    z_send(1)
    x_share(4)
    theirs(4)
    mine(3)
    x_share(5)
    z_send(2)
    theirs(5)
    mine(4)
    h_send(0)
    x_share(6)
    h_send(1)
    theirs(6)
    mine(5)
    x_share(7)
    z_send(3)
    theirs(7)
    b_send(6)
    b_send(7)
    z_send(4)
    mine(6)
    h_send(2)
    mine(7)
    z_send(5)
    b_share(0)
    h_forward(0)
    z_send(6)
    h_send(3)
    h_forward(1)
    b_forward(6)
    z_send(7)
    h_send(4)
    b_forward(7)
    h_forward(2)
    b_own_done()
    b_done(0)
    tile(0)
    h_send(5)
    h_send(6)
    h_forward(3)
    b_relay(6)
    tile(1)
    h_send(7)
    b_relay(7)
    h_forward(4)
    tile(2)
    h_forward(5)
    b_share(1)
    tile(3)
    h_forward(6)
    tile(4)
    tile(5)
    b_done(1)
    wait_all_sent()
    tile(6)

    copies = []
    last = tile_begin(BLOCKS - 1)
    for i in range(2):
        for k in range(2):
            part = acc[2 * i + k] + tile_term(BLOCKS - 1, 2 * i + k, last)
            ssend[2 * i + k] = (part * part).reshape(8, 32, 256).sum(axis=0) * scale
            stays = (a == i) & (c == k) & (yl == c)
            copy = pltpu.make_async_remote_copy(
                src_ref=ssend.at[2 * i + k], dst_ref=rr.at[2 * a + yl],
                send_sem=fin_sem.at[4 + 2 * i + k], recv_sem=fin_sem.at[2 * a + yl],
                device_id=dev(a=i, yl=c, c=k), device_id_type=MESH,
            )
            copies.append((stays, copy))

            @pl.when(stays)
            def _():
                rr[2 * i + k] = ssend[2 * i + k]

            @pl.when(jnp.logical_not(stays))
            def _():
                copy.start()

    for i in range(2):
        for k in range(2):

            @pl.when(jnp.logical_not((a == i) & (c == yl) & (yl == k)))
            def _():
                at = rr.at[2 * i + k]
                pltpu.make_async_copy(at, at, fin_sem.at[2 * i + k]).wait()

        o_ref[32 * i : 32 * i + 32] = rr[2 * i] + rr[2 * i + 1]
    for stays, copy in copies:

        @pl.when(jnp.logical_not(stays))
        def _():
            copy.wait_send()


def local(inputs, out_grads, basis_in, basis_out):
    scale = 1.0 / (inputs.shape[1] * lax.axis_size("ctx") * inputs.shape[0] * lax.axis_size("dp"))
    anywhere = pl.BlockSpec(memory_space=pl.ANY)
    return pl.pallas_call(
        functools.partial(kernel, scale),
        out_shape=jax.ShapeDtypeStruct((64, 256), F32),
        in_specs=[anywhere] * 4,
        out_specs=pl.BlockSpec(memory_space=pltpu.VMEM),
        scratch_shapes=[
            pltpu.VMEM((2, 4, 128, 1024), BF16),
            pltpu.VMEM((128, 1024), BF16),
            pltpu.VMEM((1024, 1024), BF16),
            pltpu.VMEM((8, 2, 256, 128), BF16),
            pltpu.VMEM((2, 2, 256, 128), BF16),
            pltpu.VMEM((8, 256, 128), BF16),
            pltpu.VMEM((8, 256, 128), BF16),
            pltpu.VMEM((8, 256, 128), F32),
            pltpu.VMEM((8, 256, 128), BF16),
            pltpu.VMEM((4, 8, 256, 128), BF16),
            pltpu.VMEM((4, 4, 1024, 256), BF16),
            pltpu.VMEM((4, 256, 256), F32),
            pltpu.VMEM((4, 32, 256), F32),
            pltpu.VMEM((4, 32, 256), F32),
            pltpu.SemaphoreType.DMA((N_SEND,)),
            pltpu.SemaphoreType.DMA((N_RECV,)),
            pltpu.SemaphoreType.DMA((8,)),
        ],
        compiler_params=pltpu.CompilerParams(
            collective_id=0, has_side_effects=True, vmem_limit_bytes=VMEM
        ),
    )(inputs, out_grads, basis_in.reshape(4, 1024, 256), basis_out)


def solution(mesh):
    return jax.shard_map(
        local,
        mesh=mesh,
        in_specs=(P("dp", "ctx", None), P("dp", "ctx", None), P(None, "ctx"), P()),
        out_specs=P("dp", "ctx"),
        check_vma=False,
    )
```

```python
import functools
import math

import jax
import jax.numpy as jnp
from jax import lax
from jax.experimental import pallas as pl
from jax.experimental.pallas import tpu as pltpu
from jax.sharding import PartitionSpec as P

MESH = pl.DeviceIdType.MESH
BF16, F32 = jnp.bfloat16, jnp.float32
BLOCKS = 8
PIECES = 8
EARLY = 6
DIRECT = (7,)
N_SEND = 12
N_RECV = 80
VMEM = 54976 << 10


def size(ref):
    return math.prod(ref.shape) * ref.dtype.itemsize


def kernel(
    scale, x_hbm, g_hbm, bi_hbm, bo_hbm, o_ref,
    xbuf, gbuf, bobuf, rbuf, rsend, psend, precv, pkeep, hz, hbuf, bbuf, acc, ssend, rr,
    send_sem, recv_sem, fin_sem,
):
    dp, ctx = lax.axis_index("dp"), lax.axis_index("ctx")
    yl, z = dp // 8, dp % 8
    a, b, c = ctx // 8, (ctx // 2) % 4, ctx % 2
    right, left, far = (b + 1) % 4, (b + 3) % 4, (b + 2) % 4
    own, partner = a * 2 + c, (1 - a) * 2 + c
    senders, receivers, sent, due = {}, {}, {}, {}

    def dev(a=a, yl=yl, z=z, b=b, c=c):
        return (yl * 8 + z, a * 8 + b * 2 + c)

    sibling = dev(c=1 - c)

    def out(kind):
        return send_sem.at[senders.setdefault(kind, len(senders))]

    def into(name):
        return recv_sem.at[receivers.setdefault(name, len(receivers))]

    def send(src, dst, to, *name):
        pltpu.make_async_remote_copy(
            src_ref=src, dst_ref=dst, send_sem=out(name[0]), recv_sem=into(name),
            device_id=to, device_id_type=MESH,
        ).start()
        sent[name[0]] = sent.get(name[0], 0) + size(src)
        due.setdefault(name, []).append(dst)

    def wait(ref, *name):
        assert size(ref) == sum(map(size, due.pop(name))), name
        pltpu.make_async_copy(ref, ref, into(name)).wait()

    def wait_sent(ref, kind):
        assert size(ref) == sent.pop(kind), kind
        pltpu.make_async_remote_copy(
            src_ref=ref, dst_ref=ref, send_sem=out(kind), recv_sem=recv_sem.at[0],
            device_id=sibling, device_id_type=MESH,
        ).wait_send()

    def local(src, dst, name):
        copy = pltpu.make_async_copy(src, dst, into(name))
        copy.start()
        return copy

    peers = [dev(b=(b + i) % 4, c=k) for i in (1, 3) for k in (0, 1)]
    peers += [dev(b=far), sibling]
    peers += [dev(z=(z + i) % 8) for i in range(1, 8)]
    peers += [
        dev(a=(a + i) % 2, yl=(yl + j) % 2, c=k)
        for i, j in ((0, 1), (1, 0), (1, 1))
        for k in (0, 1)
    ]
    barrier = pltpu.get_barrier_semaphore()
    for peer in peers:
        pl.semaphore_signal(barrier, inc=1, device_id=peer, device_id_type=MESH)
    features = pl.ds(pl.multiple_of(b * 1024, 1024), 1024)
    load_g = local(g_hbm.at[0], gbuf, "g")
    for i in range(4):
        rows = pl.ds(256 * i, 256)
        local(bo_hbm.at[rows], bobuf.at[rows], "bo")
    load_bo = pltpu.make_async_copy(bo_hbm, bobuf, into("bo"))
    load_x = pltpu.make_async_copy(x_hbm.at[0, :, features], xbuf.at[c, b], into("x"))
    load_bi = pltpu.make_async_copy(bi_hbm, bbuf.at[own], into("bi"))
    pl.semaphore_wait(barrier, len(peers))

    def at_lanes(j):
        return pl.ds(j * 128, 128)

    def at_rows(k):
        return pl.ds(pl.multiple_of(k * 32, 32), 32)

    def x_send(j):
        for to in (right, left, far):
            src = pl.ds(pl.multiple_of(to * 1024 + j * 128, 128), 128)
            send(x_hbm.at[0, :, src], xbuf.at[c, b, :, at_lanes(j)], dev(b=to), "X", j)

    def x_share(j):
        wait(xbuf.at[0, pl.ds(0, 3), :, at_lanes(j)], "X", j)
        at = (c, slice(None), slice(None), at_lanes(j))
        send(xbuf.at[at], xbuf.at[at], sibling, "XF", j)

    def b_at(k, g):
        rows = 1024 // PIECES
        return (2 * (z % 2) + k, pl.ds(g * rows, rows))

    def b_send(g):
        at = b_at(1 - yl, g)
        send(bi_hbm.at[at], bbuf.at[(own, *at)], dev(a=1 - a, yl=1 - yl), "B1", g)

    def b_forward(g):
        ref = bbuf.at[(partner, *b_at(yl, g))]
        wait(ref, "B1", g)
        send(ref, ref, dev(yl=1 - yl), "B2", g)
        send(ref, ref, dev(z=(z + 9 - 2 * yl) % 8), "BZ", int(g >= EARLY))

    def b_relay(g):
        ref = bbuf.at[(partner, *b_at(1 - yl, g))]
        wait(ref, "B2", g)
        send(ref, ref, dev(z=(z + 7 + 2 * yl) % 8), "BZ", int(g >= EARLY))

    def b_rows(h):
        rows = 1024 // PIECES
        return pl.ds(EARLY * rows, 1024 - EARLY * rows) if h else pl.ds(0, EARLY * rows)

    def b_share(h):
        wait(bbuf.at[partner, pl.ds(0, 2), b_rows(h)], "BZ", h)
        ref = bbuf.at[partner, :, b_rows(h)]
        send(ref, ref, sibling, "B3", h)

    def b_done(h):
        wait(bbuf.at[3 - own, :, b_rows(h)], "B3", h)

    def b_own_done():
        load_bi.wait()
        wait(bbuf.at[a * 2 + 1 - c], "B0")

    def b_own():
        send(bi_hbm, bbuf.at[own], sibling, "B0")

    slot = c * 4 + b

    def r_compute():
        load_g.wait()
        load_bo.wait()
        load_x.start()
        load_bi.start()
        for k in range(2):
            rot = jnp.dot(
                gbuf[...], bobuf[:, 512 * k : 512 * k + 512], preferred_element_type=F32
            )
            turned = rot.T.astype(BF16).reshape(8, 2, 32, 128)
            for h in range(2):
                rsend[k, h] = turned[:, h].reshape(256, 128)

    def half(p):
        return a if p else 1 - a

    def r_send(p):
        h = half(p)
        for i, to in ((1, right), (3, left)):
            send(rsend.at[c, h], rbuf.at[slot, h], dev(b=to), "R", p, i)
            send(rsend.at[1 - c, h], rbuf.at[slot, h], dev(b=to, c=1 - c), "R", p, i)
        send(rsend.at[1 - c, h], rbuf.at[slot, h], sibling, "R", p, 2)
        rbuf[slot, h] = rsend[c, h]

    def r_forward(p):
        h = half(p)
        for i, origin, to, first in ((1, left, right, 0), (3, right, left, 4)):
            wait(rbuf.at[pl.ds(0, 2), 0], "R", p, i)
            block = rbuf.at[first + origin, h]
            send(block, block, dev(b=to), "R", p, 2)

    def r_done(p):
        wait(rbuf.at[pl.ds(0, 3), 0], "R", p, 2)

    def product(j, h):
        lhs = jnp.concatenate([rbuf[s, h] for s in range(8)], axis=1)
        rhs = xbuf[:, :, :, j * 128 : j * 128 + 128].reshape(1024, 128)
        return jnp.dot(lhs, rhs, preferred_element_type=F32)

    def theirs(j):
        wait(xbuf.at[1 - c, :, :, at_lanes(j)], "XF", j)
        psend[j] = product(j, 1 - a).astype(BF16)
        send(psend.at[j], precv.at[j], dev(a=1 - a), "P", j)

    def mine(j):
        pkeep[j] = product(j, a)

    def z_send(j):
        wait(precv.at[j], "P", j)
        hz[j] = (pkeep[j] + precv[j].astype(F32)).astype(BF16)
        for i in (4, 3, 5, 2, 6, 1, 7):
            to = (z + i) % 8
            send(hz.at[j, at_rows(to)], hbuf.at[b, j, at_rows(z)], dev(z=to), "Z", j)
        hbuf[b, j, at_rows(z)] = hz[j, at_rows(z)]

    def h_send(j):
        wait(hbuf.at[b, j, pl.ds(0, 224)], "Z", j)
        ref = hbuf.at[b, j]
        if j in DIRECT:
            send(ref, ref, dev(b=far), "HF", j)
        for to in (right, left):
            send(ref, ref, dev(b=to), "H", j)

    def h_wait(j):
        wait(hbuf.at[pl.ds(0, 2), j], "H", j)

    def h_forward(j):
        h_wait(j)
        for origin, to, first in ((left, right, 0), (right, left, 128)):
            part = hbuf.at[origin, j, pl.ds(first, 128)]
            send(part, part, dev(b=to), "HF", j)

    def tile_begin(j):
        if j in DIRECT:
            h_wait(j)
        wait(hbuf.at[far, j], "HF", j)
        return jnp.concatenate([hbuf[x, j] for x in range(4)], axis=1)

    def tile_term(j, k, lhs):
        rhs = bbuf[k, :, j * 128 : j * 128 + 128].reshape(512, 256)
        return jnp.dot(lhs, rhs, preferred_element_type=F32)

    def tile(j):
        lhs = tile_begin(j)
        for k in range(4):
            term = tile_term(j, k, lhs)
            acc[k] = term if j == 0 else acc[k] + term

    def wait_all_sent():
        wait_sent(xbuf.at[0, pl.ds(0, 3)], "X")
        wait_sent(xbuf.at[0], "XF")
        wait_sent(rbuf.at[pl.ds(0, 7)], "R")
        wait_sent(psend, "P")
        wait_sent(hz.at[pl.ds(0, 7)], "Z")
        wait_sent(hbuf.at[pl.ds(0, 2)], "H")
        wait_sent(hbuf.at[0], "HF")
        wait_sent(bbuf.at[0], "B0")
        wait_sent(bbuf.at[0, 0], "B1")
        wait_sent(bbuf.at[0, 0], "B2")
        wait_sent(bbuf.at[0, pl.ds(0, 2)], "BZ")
        wait_sent(bbuf.at[0], "B3")

    x_send(0)
    b_send(0)
    b_send(1)
    b_send(2)
    b_send(3)
    b_send(4)
    b_send(5)
    r_compute()
    r_send(0)
    r_send(1)
    b_own()
    load_x.wait()
    x_share(0)
    b_forward(0)
    r_forward(0)
    x_send(1)
    x_send(2)
    b_forward(1)
    b_forward(2)
    b_forward(3)
    b_relay(0)
    r_forward(1)
    x_send(3)
    x_send(4)
    x_send(5)
    x_send(6)
    x_send(7)
    b_forward(4)
    b_relay(1)
    r_done(0)
    theirs(0)
    b_forward(5)
    b_relay(2)
    x_share(1)
    theirs(1)
    b_relay(3)
    x_share(2)
    theirs(2)
    b_relay(4)
    r_done(1)
    mine(0)
    mine(1)
    b_relay(5)
    z_send(0)
    x_share(3)
    theirs(3)
    mine(2)
    z_send(1)
    x_share(4)
    theirs(4)
    mine(3)
    x_share(5)
    z_send(2)
    theirs(5)
    mine(4)
    h_send(0)
    x_share(6)
    h_send(1)
    theirs(6)
    mine(5)
    x_share(7)
    z_send(3)
    b_share(0)
    theirs(7)
    b_send(6)
    b_send(7)
    z_send(4)
    mine(6)
    h_send(2)
    mine(7)
    z_send(5)
    h_forward(0)
    z_send(6)
    h_send(3)
    h_forward(1)
    b_forward(6)
    z_send(7)
    h_send(4)
    b_forward(7)
    h_forward(2)
    b_own_done()
    b_done(0)
    tile(0)
    h_send(5)
    h_send(6)
    h_forward(3)
    b_relay(6)
    tile(1)
    h_send(7)
    b_relay(7)
    h_forward(4)
    tile(2)
    h_forward(5)
    b_share(1)
    tile(3)
    h_forward(6)
    tile(4)
    tile(5)
    b_done(1)
    wait_all_sent()
    tile(6)

    copies = []
    last = tile_begin(BLOCKS - 1)
    for i in range(2):
        for k in range(2):
            part = acc[2 * i + k] + tile_term(BLOCKS - 1, 2 * i + k, last)
            ssend[2 * i + k] = (part * part).reshape(8, 32, 256).sum(axis=0) * scale
            stays = (a == i) & (c == k) & (yl == c)
            copy = pltpu.make_async_remote_copy(
                src_ref=ssend.at[2 * i + k], dst_ref=rr.at[2 * a + yl],
                send_sem=fin_sem.at[4 + 2 * i + k], recv_sem=fin_sem.at[2 * a + yl],
                device_id=dev(a=i, yl=c, c=k), device_id_type=MESH,
            )
            copies.append((stays, copy))

            @pl.when(stays)
            def _():
                rr[2 * i + k] = ssend[2 * i + k]

            @pl.when(jnp.logical_not(stays))
            def _():
                copy.start()

    for i in range(2):
        for k in range(2):

            @pl.when(jnp.logical_not((a == i) & (c == yl) & (yl == k)))
            def _():
                at = rr.at[2 * i + k]
                pltpu.make_async_copy(at, at, fin_sem.at[2 * i + k]).wait()

        o_ref[32 * i : 32 * i + 32] = rr[2 * i] + rr[2 * i + 1]
    for stays, copy in copies:

        @pl.when(jnp.logical_not(stays))
        def _():
            copy.wait_send()


def local(inputs, out_grads, basis_in, basis_out):
    scale = 1.0 / (inputs.shape[1] * lax.axis_size("ctx") * inputs.shape[0] * lax.axis_size("dp"))
    anywhere = pl.BlockSpec(memory_space=pl.ANY)
    return pl.pallas_call(
        functools.partial(kernel, scale),
        out_shape=jax.ShapeDtypeStruct((64, 256), F32),
        in_specs=[anywhere] * 4,
        out_specs=pl.BlockSpec(memory_space=pltpu.VMEM),
        scratch_shapes=[
            pltpu.VMEM((2, 4, 128, 1024), BF16),
            pltpu.VMEM((128, 1024), BF16),
            pltpu.VMEM((1024, 1024), BF16),
            pltpu.VMEM((8, 2, 256, 128), BF16),
            pltpu.VMEM((2, 2, 256, 128), BF16),
            pltpu.VMEM((8, 256, 128), BF16),
            pltpu.VMEM((8, 256, 128), BF16),
            pltpu.VMEM((8, 256, 128), F32),
            pltpu.VMEM((8, 256, 128), BF16),
            pltpu.VMEM((4, 8, 256, 128), BF16),
            pltpu.VMEM((4, 4, 1024, 256), BF16),
            pltpu.VMEM((4, 256, 256), F32),
            pltpu.VMEM((4, 32, 256), F32),
            pltpu.VMEM((4, 32, 256), F32),
            pltpu.SemaphoreType.DMA((N_SEND,)),
            pltpu.SemaphoreType.DMA((N_RECV,)),
            pltpu.SemaphoreType.DMA((8,)),
        ],
        compiler_params=pltpu.CompilerParams(
            collective_id=0, has_side_effects=True, vmem_limit_bytes=VMEM
        ),
    )(inputs, out_grads, basis_in.reshape(4, 1024, 256), basis_out)


def solution(mesh):
    return jax.shard_map(
        local,
        mesh=mesh,
        in_specs=(P("dp", "ctx", None), P("dp", "ctx", None), P(None, "ctx"), P()),
        out_specs=P("dp", "ctx"),
        check_vma=False,
    )
```
